256 devices in a mesh: grp: 16 (over z_lo, y, core), ctx: 16 (over x, z_hi).
Axes of the slice: x: 4, y: 4, z: 8 (z_hi: 4, z_lo: 2; z = z_hi * 2 + z_lo), core: 2. Of those that a mesh axis runs over, the one named last changes fastest.
Arguments:
- history: bfloat16 [16, 3072, 1024], P('grp', 'ctx'), may hold values from -6 to 6
- candidates: bfloat16 [16, 4096, 1024], P('grp', 'ctx'), may hold values from -6 to 6
- lengths: int32 [16], P('grp'), may hold values from 768 to 3072, as said below
- block_order: int32 [16, 16], P('grp'), may hold values from 0 to 15, each once within a row
- targets: int32 [16, 4096], P('grp', 'ctx'), may hold values from 0 to 7
- projection: bfloat16 [1024, 4096], replicated, may hold values from -0.1875 to 0.1875
- output_weight: bfloat16 [1024, 1024], P('grp'), may hold values from -0.1875 to 0.1875
- task_weight: bfloat16 [1024, 8], replicated, may hold values from -0.1875 to 0.1875
Outputs:
- layer_output: bfloat16 [16, 3072, 1024], P('grp', 'ctx')
- task_logprob: float32 [16, 4096], P('grp', 'ctx')
The draws below stay inside these ranges and needn't reach their ends.
Inputs may be any that keep to these rules, and one draw needn't show every extreme that they name: `lengths`: each user's history holds 3072 stored rows, the live ones being positions below its length; some user has all 3072 live. `block_order`: each row is a permutation of 0 to 16 - 1.
All inputs are finite; a program needn't handle non-finite values.
Results may differ from the reference program's by a relative error of at most 0.005.
Values may be sent and summed in bfloat16 or wider, within the bound.
A program may use at most 128 MiB of HBM per device.

```python
import jax
import jax.numpy as jnp
from jax import lax

D = 1024
HEADS = 8
TASKS = 8
H_DEV = 192
HEAD_DIM = 128
USERS = 16
HIST = 3072
CAND = 4096
N_CTX = 16


def draw_lengths(key, part):
    key = jax.random.fold_in(key, 7)
    first_key, second_key = jax.random.split(key)
    drawn = jax.random.randint(first_key, (USERS,), HIST // 4, HIST + 1)
    fullest = jax.random.randint(second_key, (), 0, USERS)
    drawn = jnp.where(jnp.arange(USERS) == fullest, HIST, drawn)
    return drawn.astype(jnp.int32)


def place_ends(values, rng, smallest, top_value):
    shape = values.shape
    spot = [jax.random.randint(jax.random.fold_in(rng, axis), (), 0, shape[axis]) for axis in range(len(shape))]
    values = values.at[tuple(spot)].set(smallest)
    longest = shape.index(max(shape))
    spot[longest] = (spot[longest] + 1) % shape[longest]
    return values.at[tuple(spot)].set(top_value)


def level_of(rng, dims, pieces, least, largest):
    factor_of, own = 1.0, jax.random.fold_in(rng, 6)
    for dim, blocks in pieces:
        draws = jnp.exp(jax.random.uniform(jax.random.fold_in(own, dim), (blocks,), jnp.float32, least / len(pieces), largest / len(pieces)))
        factor_of = factor_of * jnp.repeat(draws, dims[dim] // blocks).reshape([-1 if axis == dim else 1 for axis in range(len(dims))])
    return factor_of


def scatter_about(key, dims, width, bound, cuts=(), held_as=jnp.bfloat16):
    values = width * jax.random.normal(key, dims, jnp.float32)
    if cuts:
        values = values * level_of(key, dims, cuts, -0.22, 0.18)
    return jnp.clip(values, -bound, bound).astype(held_as)


def setup_inputs(seed: int = 0) -> dict:
    seeds = jax.random.split(jax.random.key(seed), 9)
    history = scatter_about(seeds[0], (USERS, HIST, D), 1.0, 6.0, ((0, 16), (1, 16)))
    candidates = scatter_about(seeds[1], (USERS, CAND, D), 1.0, 6.0, ((0, 16), (1, 16)))
    lengths = draw_lengths(jax.random.fold_in(seeds[8], 71), 0)
    block_order = jax.vmap(lambda own: jax.random.permutation(own, N_CTX))(jax.random.split(seeds[3], USERS)).reshape((USERS, N_CTX)).astype(jnp.int32)
    targets = place_ends(jax.random.randint(seeds[4], (USERS, CAND), 0, TASKS), jax.random.fold_in(seeds[4], 1), 0, TASKS - 1).astype(jnp.int32)
    projection = scatter_about(seeds[5], (D, 4 * D), D ** -0.5, 0.1875)
    output_weight = scatter_about(seeds[6], (D, D), D ** -0.5, 0.1875, ((0, 16),))
    task_weight = scatter_about(seeds[7], (D, TASKS), D ** -0.5, 0.1875)
    return dict(history=history, candidates=candidates, lengths=lengths, block_order=block_order, targets=targets, projection=projection, output_weight=output_weight, task_weight=task_weight)


norm_eps = 1e-05

def layer_norm(mixed):
    centre = mixed - lax.optimization_barrier(jnp.mean(mixed, axis=-1, keepdims=True))
    spread = lax.optimization_barrier(jnp.mean(centre * centre, axis=-1, keepdims=True))
    return centre * lax.rsqrt(spread + norm_eps)

def split_heads(matrix):
    return matrix.astype(jnp.float32).reshape(matrix.shape[0], HEADS, HEAD_DIM).transpose(1, 0, 2)

def attend_reference(queries, keys, values, allowed):
    scale = HEAD_DIM ** (-0.5)

    def one_head(operands):
        query_one, key_one, value_one = operands
        scores = jnp.dot(query_one, key_one.T, precision=lax.Precision.HIGHEST) * scale
        weights = jnp.where(allowed, jax.nn.silu(scores), 0.0).astype(jnp.bfloat16)
        weights = lax.optimization_barrier(weights).astype(jnp.float32)
        return jnp.dot(weights, value_one, precision=lax.Precision.HIGHEST)
    mixed = lax.map(one_head, (split_heads(queries), split_heads(keys), split_heads(values)))
    return mixed.transpose(1, 0, 2).reshape(queries.shape[0], HEADS * HEAD_DIM)

def self_reference(queries, keys, values):
    scale = HEAD_DIM ** (-0.5)
    count = queries.shape[0]
    head_scores = lax.optimization_barrier(jnp.sum((queries.astype(jnp.float32) * keys.astype(jnp.float32)).reshape(count, HEADS, HEAD_DIM), axis=-1)) * scale
    weights = jax.nn.silu(head_scores).astype(jnp.bfloat16)
    weights = lax.optimization_barrier(weights).astype(jnp.float32)
    return (weights[:, :, None] * values.astype(jnp.float32).reshape(count, HEADS, HEAD_DIM)).reshape(count, HEADS * HEAD_DIM)

def reference(history, candidates, lengths, block_order, targets, projection, output_weight, task_weight):

    def one_user(operands):
        hist_rows, cand_rows, limit, order_row, target_row = operands
        stored = jnp.arange(HIST, dtype=jnp.int32)
        positions = order_row[stored // H_DEV].astype(jnp.int32) * H_DEV + stored % H_DEV
        live = positions < limit
        hist_proj = jax.nn.silu(jnp.dot(hist_rows, projection, preferred_element_type=jnp.float32)).astype(jnp.bfloat16)
        cand_proj = jax.nn.silu(jnp.dot(cand_rows, projection, preferred_element_type=jnp.float32)).astype(jnp.bfloat16)
        hist_gate = hist_proj[:, :D]
        hist_value = hist_proj[:, D:2 * D]
        hist_query = hist_proj[:, 2 * D:3 * D]
        hist_key = hist_proj[:, 3 * D:]
        cand_gate = cand_proj[:, :D]
        cand_value = cand_proj[:, D:2 * D]
        cand_query = cand_proj[:, 2 * D:3 * D]
        cand_key = cand_proj[:, 3 * D:]
        causal = (positions[None, :] <= positions[:, None]) & live[None, :]
        hist_mix = attend_reference(hist_query, hist_key, hist_value, causal)
        hist_gated = (layer_norm(hist_mix) * hist_gate.astype(jnp.float32)).astype(jnp.bfloat16)
        hist_out = hist_rows.astype(jnp.float32) + jnp.dot(hist_gated, output_weight, preferred_element_type=jnp.float32)
        hist_out = jnp.where(live[:, None], hist_out, 0.0).astype(jnp.bfloat16)
        cand_allowed = jnp.broadcast_to(live[None, :], (CAND, HIST))
        cand_mix = attend_reference(cand_query, hist_key, hist_value, cand_allowed)
        cand_mix = cand_mix + self_reference(cand_query, cand_key, cand_value)
        cand_gated = (layer_norm(cand_mix) * cand_gate.astype(jnp.float32)).astype(jnp.bfloat16)
        cand_out = (cand_rows.astype(jnp.float32) + jnp.dot(cand_gated, output_weight, preferred_element_type=jnp.float32)).astype(jnp.bfloat16)
        logits = jnp.dot(cand_out, task_weight, preferred_element_type=jnp.float32)
        picked = lax.optimization_barrier(jnp.sum(jnp.where(target_row[:, None] == jnp.arange(TASKS, dtype=jnp.int32)[None, :], logits, 0.0), axis=1))
        return (hist_out, -jax.nn.softplus(-picked))
    layer_output, task_logprob = lax.map(one_user, (history, candidates, lengths, block_order, targets))
    return (layer_output, task_logprob)
```

```python
import functools

import jax
import jax.numpy as jnp
from jax import lax
from jax.experimental import pallas as pl
from jax.experimental.pallas import tpu as pltpu
from jax.sharding import PartitionSpec as P

HEADS = 8
NORM_EPS = 1e-05
ROUNDS = 6
F32, BF16 = jnp.float32, jnp.bfloat16
MESH = pl.DeviceIdType.MESH


def silu_of_double(half):
    return half + half * jnp.tanh(half)


def layer_norm(mixed):
    centre = mixed - jnp.mean(mixed, axis=-1, keepdims=True)
    spread = jnp.mean(centre * centre, axis=-1, keepdims=True)
    return centre * lax.rsqrt(spread + NORM_EPS)


def kernel(
    hist, cand, lengths, order, proj, out_weight, task_t,
    hist_out, logits_out,
    w, ow, hb, cb, xb, kv, pj, acc, gated, stage, mloc, mb, lbuf,
    w_sem, hb_send, hb_recv, cb_send, cb_recv, mb_send, mb_recv,
    h_send, h_recv, z_send, z_recv, e_send, e_recv, d_send, d_recv,
    ow_send, ow_recv, ow_local, ret_send, ret_recv,
):
    rows = hb.shape[0]
    cands = cb.shape[0]
    width = hb.shape[1]
    part = rows // ROUNDS
    half = part // 2
    column = 4 * part
    mine = 2 * column
    head = width // HEADS
    half_scale = 0.5 * head ** (-0.5)

    g = lax.axis_index("grp")
    c = lax.axis_index("ctx")
    core = lax.rem(g, 2)
    pair = g - core
    zlo = g // 8
    y = lax.rem(g // 2, 4)
    x = c // 4
    z = lax.rem(c, 4)
    swapped = lax.rem(x // 2 + core, 2)
    home_core = lax.rem(core + swapped, 2)
    home_x = x + swapped * (3 - 2 * x)
    z_up = lax.rem(z + 1, 4)
    z_down = lax.rem(z + 3, 4)
    z_far = lax.rem(z + 2, 4)

    swap = (pair + home_core, home_x * 4 + z)
    home_up = (pair + home_core, home_x * 4 + z_up)
    home_down = (pair + home_core, home_x * 4 + z_down)
    col_up = (g, x * 4 + z_up)
    col_down = (g, x * 4 + z_down)
    across = (g, (x + 1 - 2 * lax.rem(x, 2)) * 4 + z)
    sibling = (pair + 1 - core, c)
    z_pair = ((1 - zlo) * 8 + y * 2 + core, c)
    y_others = [(zlo * 8 + lax.rem(y + i, 4) * 2 + core, c) for i in (1, 2, 3)]

    def remote(src, dst, send, recv, to):
        return pltpu.make_async_remote_copy(
            src_ref=src, dst_ref=dst, send_sem=send, recv_sem=recv, device_id=to, device_id_type=MESH
        )

    def arrived(ref, sem):
        pltpu.make_async_copy(ref, ref, sem).wait()

    barrier = pltpu.get_barrier_semaphore()
    greeted = [home_up, home_down, across, sibling, z_pair, *y_others]
    for other in greeted:
        pl.semaphore_signal(barrier, inc=1, device_id=other, device_id_type=MESH)

    @pl.when(swapped == 1)
    def _():
        pl.semaphore_signal(barrier, inc=1, device_id=swap, device_id_type=MESH)
        pl.semaphore_signal(barrier, inc=1, device_id=col_up, device_id_type=MESH)
        pl.semaphore_signal(barrier, inc=1, device_id=col_down, device_id_type=MESH)

    w_copy = pltpu.make_async_copy(proj, w, w_sem)
    w_copy.start()
    ow_own = pltpu.make_async_copy(out_weight, ow.at[zlo * 4 + y, core], ow_local)
    ow_own.start()

    lane = lax.broadcasted_iota(jnp.int32, (8, 2 * mine), 1)
    slot = lane // part
    own_block = order[0, c]
    limit = lengths[0]
    block = jnp.zeros_like(lane)
    x_pair = x + 1 - 2 * lax.rem(x, 2)
    columns = (x, x_pair, 3 - x, 3 - x_pair)
    for i, source in enumerate(columns):
        for zs in range(4):
            block = jnp.where(slot == 4 * i + zs, order[0, source * 4 + zs], block)
    row_id = lax.broadcasted_iota(jnp.int32, (8, 2 * mine), 0)
    first = block * rows + lax.rem(lane, part)
    causal = jnp.where(row_id == 0, block, -1) < own_block
    for r in range(ROUNDS):
        live = first + r * part < limit
        mloc[r] = jnp.where(live & causal, half_scale, 0.0)

    pl.semaphore_wait(barrier, len(greeted) + 3 * swapped)

    def hist_part(r):
        return hist.at[0, pl.ds(pl.multiple_of(r * part, part), part)]

    def slot_of(zs):
        return pl.ds(pl.multiple_of(zs * part, part), part)

    def send_up(r):
        return remote(hist_part(r), xb.at[r, 0, slot_of(z)], h_send.at[r, 0], h_recv.at[r, 0], home_up)

    def send_down(r):
        return remote(hist_part(r), xb.at[r, 0, slot_of(z)], h_send.at[r, 1], h_recv.at[r, 1], home_down)

    hb_remote = remote(hist.at[0], hb, hb_send, hb_recv, swap)
    cb_remote = remote(cand.at[0], cb, cb_send, cb_recv, swap)
    mb_remote = remote(mloc, mb, mb_send, mb_recv, swap)

    @pl.when(swapped == 1)
    def _():
        hb_remote.start()
        cb_remote.start()
        mb_remote.start()

    @pl.when(swapped == 0)
    def _():
        pltpu.make_async_copy(hist.at[0], hb, hb_recv).start()
        pltpu.make_async_copy(cand.at[0], cb, cb_recv).start()
        pltpu.make_async_copy(mloc, mb, mb_recv).start()

    @pl.loop(0, ROUNDS)
    def _(r):
        send_up(r).start()
        send_down(r).start()

    ow_mine = out_weight
    ow_slot = ow.at[zlo * 4 + y, core]
    ow_first = [remote(ow_mine, ow_slot, ow_send.at[0], ow_recv.at[0], z_pair)]
    for i in range(3):
        ow_first.append(remote(ow_mine, ow_slot, ow_send.at[1 + i], ow_recv.at[1 + i], y_others[i]))
    for copy in ow_first:
        copy.start()

    def ow_from(zl, yy):
        return ow.at[zl * 4 + yy, core]

    ow_other = ow_from(1 - zlo, y)
    ow_second = [
        remote(ow_other, ow_other, ow_send.at[4 + i], ow_recv.at[4 + i], y_others[i]) for i in range(3)
    ]
    ow_third = remote(ow.at[:, core], ow.at[:, core], ow_send.at[7], ow_recv.at[7], sibling)

    def own_part(r):
        return hb.at[pl.ds(pl.multiple_of(r * part, part), part)]

    def give(r, k, src, zs):
        return remote(src, xb.at[r, 1, slot_of(zs)], e_send.at[r, k], e_recv.at[r, k], across)

    def give_own(r):
        return give(r, 0, own_part(r), z)

    def give_down(r):
        return give(r, 1, xb.at[r, 0, slot_of(z_down)], z_down)

    def give_up(r):
        return give(r, 2, xb.at[r, 0, slot_of(z_up)], z_up)

    def give_far(r):
        return give(r, 3, xb.at[r, 0, slot_of(z_far)], z_far)

    def half_of(zs, i):
        return pl.ds(pl.multiple_of(zs * part + i * half, half), half)

    def pass_up(r):
        ref = xb.at[r, 0, half_of(z_down, 0)]
        return remote(ref, ref, z_send.at[r, 0], z_recv.at[r, 0], col_up)

    def pass_down(r):
        ref = xb.at[r, 0, half_of(z_up, 1)]
        return remote(ref, ref, z_send.at[r, 1], z_recv.at[r, 1], col_down)

    def near_blocks(r):
        arrived(xb.at[r, 0, slot_of(z_down)], h_recv.at[r, 0])
        pass_up(r).start()
        give_down(r).start()
        arrived(xb.at[r, 0, slot_of(z_up)], h_recv.at[r, 1])
        pass_down(r).start()
        give_up(r).start()

    def far_block(r):
        arrived(xb.at[r, 0, half_of(z_far, 0)], z_recv.at[r, 0])
        arrived(xb.at[r, 0, half_of(z_far, 1)], z_recv.at[r, 1])
        give_far(r).start()

    def share(r):
        return remote(kv.at[r, 0], kv.at[r, 1], d_send.at[r], d_recv.at[r], sibling)

    def project(src, base, count):
        for j in range(0, 4 * width, 256):
            p = jnp.dot(src[...], w[:, j : j + 256], preferred_element_type=F32)
            pj[base : base + count, j : j + 256] = silu_of_double(0.5 * p).astype(BF16)

    def keys_values(r):
        for k, zs in enumerate((z, z_down, z_up, z_far)):
            arrived(xb.at[r, 1, slot_of(zs)], e_recv.at[r, k])
        block_rows = xb[r].reshape(mine, width)
        for j in range(0, 2 * width, 256):
            start = width + j if j < width else 2 * width + j
            p = jnp.dot(block_rows, w[:, start : start + 256], preferred_element_type=F32)
            kv[r, 0, :, j : j + 256] = silu_of_double(0.5 * p).astype(BF16)
        share(r).start()

    def attend(r, base, count, mask_row):
        for h in range(HEADS):
            cols = slice(h * head, (h + 1) * head)
            key_cols = slice(width + h * head, width + (h + 1) * head)
            keys = kv[r, :, :, key_cols].reshape(2 * mine, head)
            values = kv[r, :, :, cols].reshape(2 * mine, head)
            q = pj[base : base + count, 2 * width + h * head : 2 * width + (h + 1) * head]
            s = lax.dot_general(q, keys, (((1,), (1,)), ((), ())), preferred_element_type=F32)
            if mask_row is None:
                t = jnp.concatenate(
                    [s[:rows] * mb[r, 0:1, :], s[rows:] * mb[r, 1:2, :]], axis=0
                )
            else:
                t = s * mb[r, mask_row : mask_row + 1, :]
            weights = silu_of_double(t).astype(BF16)
            acc[base : base + count, cols] += jnp.dot(weights, values, preferred_element_type=F32)

    arrived(hb, hb_recv)

    @pl.loop(0, ROUNDS)
    def _(r):
        give_own(r).start()
        xb[r, 0, slot_of(z), :] = hb[pl.ds(pl.multiple_of(r * part, part), part), :]

    w_copy.wait()
    project(hb, 0, rows)
    near_blocks(0)

    tri = lax.broadcasted_iota(jnp.int32, (rows, rows), 1) <= lax.broadcasted_iota(
        jnp.int32, (rows, rows), 0
    )
    for h in range(HEADS):
        cols = slice(h * head, (h + 1) * head)
        q = pj[0:rows, 2 * width + h * head : 2 * width + (h + 1) * head]
        k = pj[0:rows, 3 * width + h * head : 3 * width + (h + 1) * head]
        v = pj[0:rows, width + h * head : width + (h + 1) * head]
        s = lax.dot_general(q, k, (((1,), (1,)), ((), ())), preferred_element_type=F32)
        t = jnp.where(tri, s * half_scale, 0.0)
        acc[0:rows, cols] = jnp.dot(
            silu_of_double(t).astype(BF16), v, preferred_element_type=F32
        )

    arrived(cb, cb_recv)
    project(cb, rows, cands)
    near_blocks(1)
    for h in range(HEADS):
        cols = slice(h * head, (h + 1) * head)
        q = pj[rows:, 2 * width + h * head : 2 * width + (h + 1) * head].astype(F32)
        k = pj[rows:, 3 * width + h * head : 3 * width + (h + 1) * head].astype(F32)
        v = pj[rows:, width + h * head : width + (h + 1) * head].astype(F32)
        t = jnp.sum(q * k, axis=1, keepdims=True) * half_scale
        acc[rows:, cols] = silu_of_double(t).astype(BF16).astype(F32) * v
    far_block(0)
    arrived(mb, mb_recv)
    keys_values(0)

    arrived(ow_other, ow_recv.at[0])
    for copy in ow_second:
        copy.start()

    @pl.loop(1, ROUNDS)
    def _(r):
        @pl.when(r + 1 < ROUNDS)
        def _():
            near_blocks(r + 1)

        far_block(r)
        arrived(kv.at[r - 1, 1], d_recv.at[r - 1])
        attend(r - 1, 0, rows + cands, None)
        keys_values(r)

    for i in range(3):
        yy = lax.rem(y + 3 - i, 4)
        arrived(ow_from(zlo, yy), ow_recv.at[1 + i])
        arrived(ow_from(1 - zlo, yy), ow_recv.at[4 + i])
    ow_own.wait()
    ow_third.start()

    def finish(base, count):
        for j in range(base, base + count, 64):
            rows_of = slice(j, j + 64)
            gate = pj[rows_of, 0:width].astype(F32)
            gated[rows_of, :] = (layer_norm(acc[rows_of, :]) * gate).astype(BF16)

    last = ROUNDS - 1
    arrived(kv.at[last, 1], d_recv.at[last])
    attend(last, 0, rows, 0)
    finish(0, rows)
    arrived(ow.at[:, 1 - core], ow_recv.at[7])

    def branch(base, count, j):
        weight = ow[:, :, :, j : j + 256].reshape(width, 256)
        return jnp.dot(gated[base : base + count, :], weight, preferred_element_type=F32)

    for j in range(0, width, 256):
        mixed = hb[:, j : j + 256].astype(F32) + branch(0, rows, j)
        stage[:, j : j + 256] = mixed.astype(BF16)

    hist_back = remote(stage, hist_out.at[0], ret_send.at[0], ret_recv.at[0], swap)

    @pl.when(swapped == 1)
    def _():
        hist_back.start()

    @pl.when(swapped == 0)
    def _():
        pltpu.make_async_copy(stage, hist_out.at[0], ret_recv.at[0]).start()

    attend(last, rows, cands, 1)
    finish(rows, cands)
    for j in range(0, width, 256):
        mixed = cb[:, j : j + 256].astype(F32) + branch(rows, cands, j)
        cb[:, j : j + 256] = mixed.astype(BF16)
    lbuf[...] = lax.dot_general(
        task_t[...], cb[...], (((1,), (1,)), ((), ())), preferred_element_type=F32
    )
    logits_back = remote(lbuf, logits_out, ret_send.at[1], ret_recv.at[1], swap)

    @pl.when(swapped == 1)
    def _():
        logits_back.start()

    @pl.when(swapped == 0)
    def _():
        pltpu.make_async_copy(lbuf, logits_out, ret_recv.at[1]).start()

    @pl.loop(0, ROUNDS)
    def _(r):
        send_up(r).wait_send()
        send_down(r).wait_send()
        pass_up(r).wait_send()
        pass_down(r).wait_send()
        give_own(r).wait_send()
        give_down(r).wait_send()
        give_up(r).wait_send()
        give_far(r).wait_send()
        share(r).wait_send()

    for copy in (*ow_first, *ow_second, ow_third):
        copy.wait_send()

    @pl.when(swapped == 1)
    def _():
        hb_remote.wait_send()
        cb_remote.wait_send()
        mb_remote.wait_send()
        hist_back.wait_send()
        logits_back.wait_send()

    arrived(hist_out.at[0], ret_recv.at[0])
    arrived(logits_out, ret_recv.at[1])


def local(
    history, candidates, lengths, block_order, targets, projection, output_weight, task_weight
):
    rows, width = history.shape[1], history.shape[2]
    cands = candidates.shape[1]
    tasks = task_weight.shape[1]
    part = rows // ROUNDS
    mine = 8 * part
    any_space = pl.BlockSpec(memory_space=pl.ANY)
    smem = pl.BlockSpec(memory_space=pltpu.SMEM)
    vmem = pl.BlockSpec(memory_space=pltpu.VMEM)
    dma = pltpu.SemaphoreType.DMA
    hist_raw, logits = pl.pallas_call(
        kernel,
        out_shape=(
            jax.ShapeDtypeStruct((1, rows, width), BF16),
            jax.ShapeDtypeStruct((tasks, cands), F32),
        ),
        in_specs=[any_space, any_space, smem, smem, any_space, any_space, vmem],
        out_specs=(any_space, any_space),
        scratch_shapes=[
            pltpu.VMEM((width, 4 * width), BF16),
            pltpu.VMEM((8, 2, width // 16, width), BF16),
            pltpu.VMEM((rows, width), BF16),
            pltpu.VMEM((cands, width), BF16),
            pltpu.VMEM((ROUNDS, 2, 4 * part, width), BF16),
            pltpu.VMEM((ROUNDS, 2, mine, 2 * width), BF16),
            pltpu.VMEM((rows + cands, 4 * width), BF16),
            pltpu.VMEM((rows + cands, width), F32),
            pltpu.VMEM((rows + cands, width), BF16),
            pltpu.VMEM((rows, width), BF16),
            pltpu.VMEM((ROUNDS, 8, 2 * mine), F32),
            pltpu.VMEM((ROUNDS, 8, 2 * mine), F32),
            pltpu.VMEM((tasks, cands), F32),
            dma, dma, dma, dma, dma, dma, dma,
            dma((ROUNDS, 2)), dma((ROUNDS, 2)),
            dma((ROUNDS, 2)), dma((ROUNDS, 2)),
            dma((ROUNDS, 4)), dma((ROUNDS, 4)),
            dma((ROUNDS,)), dma((ROUNDS,)),
            dma((8,)), dma((8,)), dma,
            dma((2,)), dma((2,)),
        ],
        compiler_params=pltpu.CompilerParams(
            collective_id=0, has_side_effects=True, vmem_limit_bytes=56 * 2**20
        ),
    )(history, candidates, lengths, block_order, projection, output_weight, task_weight.T)
    own = block_order[0, lax.axis_index("ctx")]
    live = own * rows + jnp.arange(rows, dtype=jnp.int32) < lengths[0]
    layer_output = jnp.where(live[None, :, None], hist_raw, jnp.zeros_like(hist_raw))
    task_ids = jnp.arange(tasks, dtype=jnp.int32)
    picked = jnp.sum(jnp.where(targets[0][None, :] == task_ids[:, None], logits, 0.0), axis=0)
    return (layer_output, (-jax.nn.softplus(-picked))[None])


def solution(mesh):
    in_specs = (
        P("grp", "ctx", None),
        P("grp", "ctx", None),
        P("grp"),
        P("grp", None),
        P("grp", "ctx"),
        P(),
        P("grp", None),
        P(),
    )
    out_specs = (P("grp", "ctx", None), P("grp", "ctx"))
    return jax.shard_map(local, mesh=mesh, in_specs=in_specs, out_specs=out_specs, check_vma=False)
```

```python
import functools

import jax
import jax.numpy as jnp
from jax import lax
from jax.experimental import pallas as pl
from jax.experimental.pallas import tpu as pltpu
from jax.sharding import PartitionSpec as P

HEADS = 8
NORM_EPS = 1e-05
ROUNDS = 6
AHEAD = 3
F32, BF16 = jnp.float32, jnp.bfloat16
MESH = pl.DeviceIdType.MESH


def silu_of_double(half):
    return half + half * jnp.tanh(half)


def layer_norm(mixed):
    centre = mixed - jnp.mean(mixed, axis=-1, keepdims=True)
    spread = jnp.mean(centre * centre, axis=-1, keepdims=True)
    return centre * lax.rsqrt(spread + NORM_EPS)


def kernel(
    hist, cand, lengths, order, targets, proj, out_weight, task_weight,
    hist_out, logprob,
    w, ow, hb, cb, xb, kv, pj, acc, gated, stage, mloc, mb, lbuf, lback, task_t,
    w_sem, hb_send, hb_recv, cb_send, cb_recv, mb_send, mb_recv,
    h_send, h_recv, z_send, z_recv, e_send, e_recv, d_send, d_recv,
    ow_send, ow_recv, ow_local, ret_send, ret_recv,
):
    rows = hb.shape[0]
    cands = cb.shape[0]
    width = hb.shape[1]
    part = rows // ROUNDS
    half = part // 2
    column = 4 * part
    mine = 2 * column
    head = width // HEADS
    half_scale = 0.5 * head ** (-0.5)

    g = lax.axis_index("grp")
    c = lax.axis_index("ctx")
    core = lax.rem(g, 2)
    pair = g - core
    zlo = g // 8
    y = lax.rem(g // 2, 4)
    x = c // 4
    z = lax.rem(c, 4)
    swapped = lax.rem(x // 2 + core, 2)
    home_core = lax.rem(core + swapped, 2)
    home_x = x + swapped * (3 - 2 * x)
    z_up = lax.rem(z + 1, 4)
    z_down = lax.rem(z + 3, 4)
    z_far = lax.rem(z + 2, 4)

    swap = (pair + home_core, home_x * 4 + z)
    col_up = (g, x * 4 + z_up)
    col_down = (g, x * 4 + z_down)
    across = (g, (x + 1 - 2 * lax.rem(x, 2)) * 4 + z)
    sibling = (pair + 1 - core, c)
    z_pair = ((1 - zlo) * 8 + y * 2 + core, c)
    y_others = [(zlo * 8 + lax.rem(y + i, 4) * 2 + core, c) for i in (1, 2, 3)]

    def remote(src, dst, send, recv, to):
        return pltpu.make_async_remote_copy(
            src_ref=src, dst_ref=dst, send_sem=send, recv_sem=recv, device_id=to, device_id_type=MESH
        )

    def arrived(ref, sem):
        pltpu.make_async_copy(ref, ref, sem).wait()

    barrier = pltpu.get_barrier_semaphore()
    greeted = [col_up, col_down, across, sibling, z_pair, *y_others]
    for other in greeted:
        pl.semaphore_signal(barrier, inc=1, device_id=other, device_id_type=MESH)

    @pl.when(swapped == 1)
    def _():
        pl.semaphore_signal(barrier, inc=1, device_id=swap, device_id_type=MESH)

    w_copy = pltpu.make_async_copy(proj, w, w_sem)
    w_copy.start()
    ow_own = pltpu.make_async_copy(out_weight, ow.at[zlo * 4 + y, core], ow_local)
    ow_own.start()

    lane = lax.broadcasted_iota(jnp.int32, (8, 2 * mine), 1)
    slot = lane // part
    own_block = order[0, c]
    limit = lengths[0]
    block = jnp.zeros_like(lane)
    x_pair = x + 1 - 2 * lax.rem(x, 2)
    columns = (x, x_pair, 3 - x, 3 - x_pair)
    for i, source in enumerate(columns):
        for zs in range(4):
            block = jnp.where(slot == 4 * i + zs, order[0, source * 4 + zs], block)
    row_id = lax.broadcasted_iota(jnp.int32, (8, 2 * mine), 0)
    first = block * rows + lax.rem(lane, part)
    causal = jnp.where(row_id == 0, block, -1) < own_block
    own_live = (limit - own_block * rows).astype(F32)
    task_t[...] = task_weight[...].astype(F32).T.astype(BF16)
    for r in range(ROUNDS):
        live = first + r * part < limit
        mloc[r] = jnp.where(row_id == 2, own_live, jnp.where(live & causal, half_scale, 0.0))

    pl.semaphore_wait(barrier, len(greeted) + swapped)

    def slot_of(zs):
        return pl.ds(pl.multiple_of(zs * part, part), part)

    def part_of(r):
        return pl.ds(pl.multiple_of(r * part, part), part)

    def fetch_remote(r):
        return remote(hist.at[0, part_of(r)], hb.at[part_of(r)], hb_send.at[r], hb_recv.at[r], swap)

    cb_remote = remote(cand.at[0], cb, cb_send, cb_recv, swap)
    mb_remote = remote(mloc, mb, mb_send, mb_recv, swap)

    @pl.when(swapped == 1)
    def _():
        for r in range(ROUNDS):
            fetch_remote(r).start()

    @pl.when(swapped == 0)
    def _():
        for r in range(ROUNDS):
            pltpu.make_async_copy(hist.at[0, part_of(r)], hb.at[part_of(r)], hb_recv.at[r]).start()
        pltpu.make_async_copy(cand.at[0], cb, cb_recv).start()
        pltpu.make_async_copy(mloc, mb, mb_recv).start()

    ow_mine = out_weight
    ow_slot = ow.at[zlo * 4 + y, core]
    ow_first = [remote(ow_mine, ow_slot, ow_send.at[0], ow_recv.at[0], z_pair)]
    for i in range(3):
        ow_first.append(remote(ow_mine, ow_slot, ow_send.at[1 + i], ow_recv.at[1 + i], y_others[i]))
    for copy in ow_first:
        copy.start()

    def ow_from(zl, yy):
        return ow.at[zl * 4 + yy, core]

    ow_other = ow_from(1 - zlo, y)
    ow_second = [
        remote(ow_other, ow_other, ow_send.at[4 + i], ow_recv.at[4 + i], y_others[i]) for i in range(3)
    ]
    ow_third = remote(ow.at[:, core], ow.at[:, core], ow_send.at[7], ow_recv.at[7], sibling)

    def own_part(r):
        return hb.at[part_of(r)]

    def send_up(r):
        return remote(own_part(r), xb.at[r, 0, slot_of(z)], h_send.at[r, 0], h_recv.at[r, 0], col_up)

    def send_down(r):
        return remote(own_part(r), xb.at[r, 0, slot_of(z)], h_send.at[r, 1], h_recv.at[r, 1], col_down)

    def send_own(r):
        send_up(r).start()
        send_down(r).start()

    def give(r, k, src, zs):
        return remote(src, xb.at[r, 1, slot_of(zs)], e_send.at[r, k], e_recv.at[r, k], across)

    def give_own(r):
        return give(r, 0, own_part(r), z)

    def give_down(r):
        return give(r, 1, xb.at[r, 0, slot_of(z_down)], z_down)

    def give_up(r):
        return give(r, 2, xb.at[r, 0, slot_of(z_up)], z_up)

    def give_far(r):
        return give(r, 3, xb.at[r, 0, slot_of(z_far)], z_far)

    def half_of(zs, i):
        return pl.ds(pl.multiple_of(zs * part + i * half, half), half)

    def pass_up(r):
        ref = xb.at[r, 0, half_of(z_down, 0)]
        return remote(ref, ref, z_send.at[r, 0], z_recv.at[r, 0], col_up)

    def pass_down(r):
        ref = xb.at[r, 0, half_of(z_up, 1)]
        return remote(ref, ref, z_send.at[r, 1], z_recv.at[r, 1], col_down)

    def up_near(r):
        ref = xb.at[r, 1, slot_of(z)]
        return remote(ref, ref, e_send.at[r, 1], e_recv.at[r, 1], col_up)

    def down_near(r):
        ref = xb.at[r, 1, slot_of(z)]
        return remote(ref, ref, e_send.at[r, 2], e_recv.at[r, 2], col_down)

    def up_far(r):
        ref = xb.at[r, 1, half_of(z_down, 0)]
        return remote(ref, ref, e_send.at[r, 3], e_recv.at[r, 3], col_up)

    def down_far(r):
        ref = xb.at[r, 1, half_of(z_up, 1)]
        return remote(ref, ref, e_send.at[r, 4], e_recv.at[r, 4], col_down)

    def near_blocks(r, across_too=True):
        arrived(xb.at[r, 0, slot_of(z_down)], h_recv.at[r, 0])
        pass_up(r).start()
        if across_too:
            give_down(r).start()
        arrived(xb.at[r, 0, slot_of(z_up)], h_recv.at[r, 1])
        pass_down(r).start()
        if across_too:
            give_up(r).start()

    def far_block(r, across_too=True):
        arrived(xb.at[r, 0, half_of(z_far, 0)], z_recv.at[r, 0])
        arrived(xb.at[r, 0, half_of(z_far, 1)], z_recv.at[r, 1])
        if across_too:
            give_far(r).start()

    def near_across(r):
        arrived(xb.at[r, 1, slot_of(z)], e_recv.at[r, 0])
        up_near(r).start()
        down_near(r).start()

    def far_across(r):
        arrived(xb.at[r, 1, slot_of(z_down)], e_recv.at[r, 1])
        up_far(r).start()
        arrived(xb.at[r, 1, slot_of(z_up)], e_recv.at[r, 2])
        down_far(r).start()

    def share(r):
        return remote(kv.at[r, 0], kv.at[r, 1], d_send.at[r], d_recv.at[r], sibling)

    def project(src, base, count):
        for j in range(0, 4 * width, 256):
            p = jnp.dot(src[...], w[:, j : j + 256], preferred_element_type=F32)
            pj[base : base + count, j : j + 256] = silu_of_double(0.5 * p).astype(BF16)

    def keys_values(r, across_too=True):
        if across_too:
            for k, zs in enumerate((z, z_down, z_up, z_far)):
                arrived(xb.at[r, 1, slot_of(zs)], e_recv.at[r, k])
        else:
            for k in range(2):
                arrived(xb.at[r, 1, half_of(z_far, k)], e_recv.at[r, 3 + k])
        block_rows = xb[r].reshape(mine, width)
        for j in range(0, 2 * width, 256):
            start = width + j if j < width else 2 * width + j
            p = jnp.dot(block_rows, w[:, start : start + 256], preferred_element_type=F32)
            kv[r, 0, :, j : j + 256] = silu_of_double(0.5 * p).astype(BF16)
        share(r).start()

    def attend(r, base, count, mask_row):
        for h in range(HEADS):
            cols = slice(h * head, (h + 1) * head)
            key_cols = slice(width + h * head, width + (h + 1) * head)
            keys = kv[r, :, :, key_cols].reshape(2 * mine, head)
            values = kv[r, :, :, cols].reshape(2 * mine, head)
            q = pj[base : base + count, 2 * width + h * head : 2 * width + (h + 1) * head]
            s = lax.dot_general(q, keys, (((1,), (1,)), ((), ())), preferred_element_type=F32)
            if mask_row is None:
                t = jnp.concatenate(
                    [s[:rows] * mb[r, 0:1, :], s[rows:] * mb[r, 1:2, :]], axis=0
                )
            else:
                t = s * mb[r, mask_row : mask_row + 1, :]
            weights = silu_of_double(t).astype(BF16)
            acc[base : base + count, cols] += jnp.dot(weights, values, preferred_element_type=F32)

    last = ROUNDS - 1
    for r in range(ROUNDS):
        arrived(own_part(r), hb_recv.at[r])
        if r < AHEAD:
            send_own(r)
        give_own(r).start()
        xb[r, 0, slot_of(z), :] = hb[r * part : (r + 1) * part, :]

    @pl.when(swapped == 1)
    def _():
        cb_remote.start()
        mb_remote.start()

    w_copy.wait()
    project(hb, 0, rows)
    near_blocks(0)
    send_own(AHEAD)

    tri = lax.broadcasted_iota(jnp.int32, (rows, rows), 1) <= lax.broadcasted_iota(
        jnp.int32, (rows, rows), 0
    )
    for h in range(HEADS):
        cols = slice(h * head, (h + 1) * head)
        q = pj[0:rows, 2 * width + h * head : 2 * width + (h + 1) * head]
        k = pj[0:rows, 3 * width + h * head : 3 * width + (h + 1) * head]
        v = pj[0:rows, width + h * head : width + (h + 1) * head]
        s = lax.dot_general(q, k, (((1,), (1,)), ((), ())), preferred_element_type=F32)
        t = jnp.where(tri, s * half_scale, 0.0)
        acc[0:rows, cols] = jnp.dot(
            silu_of_double(t).astype(BF16), v, preferred_element_type=F32
        )

    near_blocks(1)
    send_own(AHEAD + 1)
    far_block(0)
    arrived(cb, cb_recv)
    project(cb, rows, cands)
    near_blocks(2)
    send_own(AHEAD + 2)
    far_block(1)
    for h in range(HEADS):
        cols = slice(h * head, (h + 1) * head)
        q = pj[rows:, 2 * width + h * head : 2 * width + (h + 1) * head].astype(F32)
        k = pj[rows:, 3 * width + h * head : 3 * width + (h + 1) * head].astype(F32)
        v = pj[rows:, width + h * head : width + (h + 1) * head].astype(F32)
        t = jnp.sum(q * k, axis=1, keepdims=True) * half_scale
        acc[rows:, cols] = silu_of_double(t).astype(BF16).astype(F32) * v
    arrived(mb, mb_recv)
    keys_values(0)
    arrived(ow_other, ow_recv.at[0])
    for copy in ow_second:
        copy.start()

    @pl.loop(1, last)
    def _(r):
        @pl.when(r + 2 < last)
        def _():
            near_blocks(r + 2)

        @pl.when(r + 2 == last)
        def _():
            near_blocks(last, False)
            near_across(last)

        @pl.when(r + 1 < last)
        def _():
            far_block(r + 1)

        @pl.when(r + 1 == last)
        def _():
            far_block(last, False)
            far_across(last)

        keys_values(r)
        arrived(kv.at[r - 1, 1], d_recv.at[r - 1])
        attend(r - 1, 0, rows + cands, None)

    keys_values(last, False)
    arrived(kv.at[last - 1, 1], d_recv.at[last - 1])
    attend(last - 1, 0, rows + cands, None)
    for i in range(3):
        yy = lax.rem(y + 3 - i, 4)
        arrived(ow_from(zlo, yy), ow_recv.at[1 + i])
        arrived(ow_from(1 - zlo, yy), ow_recv.at[4 + i])
    ow_own.wait()
    ow_third.start()

    def finish(base, count):
        for j in range(base, base + count, 64):
            rows_of = slice(j, j + 64)
            gate = pj[rows_of, 0:width].astype(F32)
            gated[rows_of, :] = (layer_norm(acc[rows_of, :]) * gate).astype(BF16)

    arrived(kv.at[last, 1], d_recv.at[last])
    attend(last, 0, rows, 0)
    finish(0, rows)
    arrived(ow.at[:, 1 - core], ow_recv.at[7])

    def branch(base, count, j):
        weight = ow[:, :, :, j : j + 256].reshape(width, 256)
        return jnp.dot(gated[base : base + count, :], weight, preferred_element_type=F32)

    row_live = lax.broadcasted_iota(jnp.int32, (rows, 256), 0).astype(F32) < mb[0, 2:3, 0:256]
    for j in range(0, width, 256):
        mixed = hb[:, j : j + 256].astype(F32) + branch(0, rows, j)
        stage[:, j : j + 256] = jnp.where(row_live, mixed, 0.0).astype(BF16)

    hist_back = remote(stage, hist_out.at[0], ret_send.at[0], ret_recv.at[0], swap)

    @pl.when(swapped == 1)
    def _():
        hist_back.start()

    @pl.when(swapped == 0)
    def _():
        pltpu.make_async_copy(stage, hist_out.at[0], ret_recv.at[0]).start()

    attend(last, rows, cands, 1)
    finish(rows, cands)
    for j in range(0, width, 256):
        mixed = cb[:, j : j + 256].astype(F32) + branch(rows, cands, j)
        cb[:, j : j + 256] = mixed.astype(BF16)
    lbuf[...] = lax.dot_general(
        task_t[...], cb[...], (((1,), (1,)), ((), ())), preferred_element_type=F32
    )
    logits_back = remote(lbuf, lback, ret_send.at[1], ret_recv.at[1], swap)

    @pl.when(swapped == 1)
    def _():
        logits_back.start()

    @pl.when(swapped == 0)
    def _():
        pltpu.make_async_copy(lbuf, lback, ret_recv.at[1]).start()

    @pl.loop(0, ROUNDS)
    def _(r):
        send_up(r).wait_send()
        send_down(r).wait_send()
        pass_up(r).wait_send()
        pass_down(r).wait_send()
        give_own(r).wait_send()
        share(r).wait_send()

        @pl.when(r < last)
        def _():
            give_down(r).wait_send()
            give_up(r).wait_send()
            give_far(r).wait_send()

    up_near(last).wait_send()
    down_near(last).wait_send()
    up_far(last).wait_send()
    down_far(last).wait_send()

    for copy in (*ow_first, *ow_second, ow_third):
        copy.wait_send()

    @pl.when(swapped == 1)
    def _():
        for r in range(ROUNDS):
            fetch_remote(r).wait_send()
        cb_remote.wait_send()
        mb_remote.wait_send()
        hist_back.wait_send()
        logits_back.wait_send()

    arrived(lback, ret_recv.at[1])
    task_id = lax.broadcasted_iota(jnp.int32, lback.shape, 0)
    picked = jnp.sum(jnp.where(task_id == targets[...], lback[...], 0.0), axis=0, keepdims=True)
    logprob[...] = jnp.minimum(picked, 0.0) - jnp.log1p(jnp.exp(-jnp.abs(picked)))
    arrived(hist_out.at[0], ret_recv.at[0])


def local(
    history, candidates, lengths, block_order, targets, projection, output_weight, task_weight
):
    rows, width = history.shape[1], history.shape[2]
    cands = candidates.shape[1]
    tasks = task_weight.shape[1]
    part = rows // ROUNDS
    mine = 8 * part
    any_space = pl.BlockSpec(memory_space=pl.ANY)
    smem = pl.BlockSpec(memory_space=pltpu.SMEM)
    vmem = pl.BlockSpec(memory_space=pltpu.VMEM)
    dma = pltpu.SemaphoreType.DMA
    return pl.pallas_call(
        kernel,
        out_shape=(
            jax.ShapeDtypeStruct((1, rows, width), BF16),
            jax.ShapeDtypeStruct((1, cands), F32),
        ),
        in_specs=[any_space, any_space, smem, smem, vmem, any_space, any_space, vmem],
        out_specs=(any_space, vmem),
        scratch_shapes=[
            pltpu.VMEM((width, 4 * width), BF16),
            pltpu.VMEM((8, 2, width // 16, width), BF16),
            pltpu.VMEM((rows, width), BF16),
            pltpu.VMEM((cands, width), BF16),
            pltpu.VMEM((ROUNDS, 2, 4 * part, width), BF16),
            pltpu.VMEM((ROUNDS, 2, mine, 2 * width), BF16),
            pltpu.VMEM((rows + cands, 4 * width), BF16),
            pltpu.VMEM((rows + cands, width), F32),
            pltpu.VMEM((rows + cands, width), BF16),
            pltpu.VMEM((rows, width), BF16),
            pltpu.VMEM((ROUNDS, 8, 2 * mine), F32),
            pltpu.VMEM((ROUNDS, 8, 2 * mine), F32),
            pltpu.VMEM((tasks, cands), F32),
            pltpu.VMEM((tasks, cands), F32),
            pltpu.VMEM((tasks, width), BF16),
            dma, dma((ROUNDS,)), dma((ROUNDS,)), dma, dma, dma, dma,
            dma((ROUNDS, 2)), dma((ROUNDS, 2)),
            dma((ROUNDS, 2)), dma((ROUNDS, 2)),
            dma((ROUNDS, 5)), dma((ROUNDS, 5)),
            dma((ROUNDS,)), dma((ROUNDS,)),
            dma((8,)), dma((8,)), dma,
            dma((2,)), dma((2,)),
        ],
        compiler_params=pltpu.CompilerParams(
            collective_id=0, has_side_effects=True, vmem_limit_bytes=56 * 2**20
        ),
    )(history, candidates, lengths, block_order, targets, projection, output_weight, task_weight)


def solution(mesh):
    in_specs = (
        P("grp", "ctx", None),
        P("grp", "ctx", None),
        P("grp"),
        P("grp", None),
        P("grp", "ctx"),
        P(),
        P("grp", None),
        P(),
    )
    out_specs = (P("grp", "ctx", None), P("grp", "ctx"))
    return jax.shard_map(local, mesh=mesh, in_specs=in_specs, out_specs=out_specs, check_vma=False)
```

```python
import functools

import jax
import jax.numpy as jnp
from jax import lax
from jax.experimental import pallas as pl
from jax.experimental.pallas import tpu as pltpu
from jax.sharding import PartitionSpec as P

HEADS = 8
NORM_EPS = 1e-05
ROUNDS = 6
AHEAD = 2
F32, BF16 = jnp.float32, jnp.bfloat16
MESH = pl.DeviceIdType.MESH


def silu_of_double(half):
    return half + half * jnp.tanh(half)


def layer_norm(mixed):
    centre = mixed - jnp.mean(mixed, axis=-1, keepdims=True)
    spread = jnp.mean(centre * centre, axis=-1, keepdims=True)
    return centre * lax.rsqrt(spread + NORM_EPS)


def kernel(
    hist, cand, lengths, order, targets, proj, out_weight, task_t,
    hist_out, logprob,
    w, ow, hb, cb, xb, kv, pj, acc, gated, stage, mloc, mb, lbuf, lback,
    w_sem, hb_send, hb_recv, cb_send, cb_recv, mb_send, mb_recv,
    h_send, h_recv, z_send, z_recv, e_send, e_recv, d_send, d_recv,
    ow_send, ow_recv, ow_local, ret_send, ret_recv,
):
    rows = hb.shape[0]
    cands = cb.shape[0]
    width = hb.shape[1]
    part = rows // ROUNDS
    half = part // 2
    column = 4 * part
    mine = 2 * column
    head = width // HEADS
    half_scale = 0.5 * head ** (-0.5)

    g = lax.axis_index("grp")
    c = lax.axis_index("ctx")
    core = lax.rem(g, 2)
    pair = g - core
    zlo = g // 8
    y = lax.rem(g // 2, 4)
    x = c // 4
    z = lax.rem(c, 4)
    swapped = lax.rem(x // 2 + core, 2)
    home_core = lax.rem(core + swapped, 2)
    home_x = x + swapped * (3 - 2 * x)
    z_up = lax.rem(z + 1, 4)
    z_down = lax.rem(z + 3, 4)
    z_far = lax.rem(z + 2, 4)

    swap = (pair + home_core, home_x * 4 + z)
    col_up = (g, x * 4 + z_up)
    col_down = (g, x * 4 + z_down)
    across = (g, (x + 1 - 2 * lax.rem(x, 2)) * 4 + z)
    sibling = (pair + 1 - core, c)
    z_pair = ((1 - zlo) * 8 + y * 2 + core, c)
    y_others = [(zlo * 8 + lax.rem(y + i, 4) * 2 + core, c) for i in (1, 2, 3)]

    def remote(src, dst, send, recv, to):
        return pltpu.make_async_remote_copy(
            src_ref=src, dst_ref=dst, send_sem=send, recv_sem=recv, device_id=to, device_id_type=MESH
        )

    def arrived(ref, sem):
        pltpu.make_async_copy(ref, ref, sem).wait()

    barrier = pltpu.get_barrier_semaphore()
    greeted = [col_up, col_down, across, sibling, z_pair, *y_others]
    for other in greeted:
        pl.semaphore_signal(barrier, inc=1, device_id=other, device_id_type=MESH)

    @pl.when(swapped == 1)
    def _():
        pl.semaphore_signal(barrier, inc=1, device_id=swap, device_id_type=MESH)

    w_copy = pltpu.make_async_copy(proj, w, w_sem)
    w_copy.start()
    ow_own = pltpu.make_async_copy(out_weight, ow.at[zlo * 4 + y, core], ow_local)
    ow_own.start()

    lane = lax.broadcasted_iota(jnp.int32, (8, 2 * mine), 1)
    slot = lane // part
    own_block = order[0, c]
    limit = lengths[0, 0]
    block = jnp.zeros_like(lane)
    x_pair = x + 1 - 2 * lax.rem(x, 2)
    columns = (x, x_pair, 3 - x, 3 - x_pair)
    for i, source in enumerate(columns):
        for zs in range(4):
            block = jnp.where(slot == 4 * i + zs, order[0, source * 4 + zs], block)
    row_id = lax.broadcasted_iota(jnp.int32, (8, 2 * mine), 0)
    first = block * rows + lax.rem(lane, part)
    causal = jnp.where(row_id == 0, block, -1) < own_block
    own_live = (limit - own_block * rows).astype(F32)
    for r in range(ROUNDS):
        live = first + r * part < limit
        mloc[r] = jnp.where(row_id == 2, own_live, jnp.where(live & causal, half_scale, 0.0))

    pl.semaphore_wait(barrier, len(greeted) + swapped)

    def slot_of(zs):
        return pl.ds(pl.multiple_of(zs * part, part), part)

    def part_of(r):
        return pl.ds(pl.multiple_of(r * part, part), part)

    def fetch_remote(r):
        return remote(hist.at[0, part_of(r)], hb.at[part_of(r)], hb_send.at[r], hb_recv.at[r], swap)

    cb_remote = remote(cand.at[0], cb, cb_send, cb_recv, swap)
    mb_remote = remote(mloc, mb, mb_send, mb_recv, swap)

    @pl.when(swapped == 1)
    def _():
        for r in range(ROUNDS):
            fetch_remote(r).start()

    @pl.when(swapped == 0)
    def _():
        for r in range(ROUNDS):
            pltpu.make_async_copy(hist.at[0, part_of(r)], hb.at[part_of(r)], hb_recv.at[r]).start()
        pltpu.make_async_copy(cand.at[0], cb, cb_recv).start()
        pltpu.make_async_copy(mloc, mb, mb_recv).start()

    ow_mine = out_weight
    ow_slot = ow.at[zlo * 4 + y, core]
    ow_first = [remote(ow_mine, ow_slot, ow_send.at[0], ow_recv.at[0], z_pair)]
    for i in range(3):
        ow_first.append(remote(ow_mine, ow_slot, ow_send.at[1 + i], ow_recv.at[1 + i], y_others[i]))
    for copy in ow_first:
        copy.start()

    def ow_from(zl, yy):
        return ow.at[zl * 4 + yy, core]

    ow_other = ow_from(1 - zlo, y)
    ow_second = [
        remote(ow_other, ow_other, ow_send.at[4 + i], ow_recv.at[4 + i], y_others[i]) for i in range(3)
    ]
    ow_third = remote(ow.at[:, core], ow.at[:, core], ow_send.at[7], ow_recv.at[7], sibling)

    def own_part(r):
        return hb.at[part_of(r)]

    def send_up(r):
        return remote(own_part(r), xb.at[r, 0, slot_of(z)], h_send.at[r, 0], h_recv.at[r, 0], col_up)

    def send_down(r):
        return remote(own_part(r), xb.at[r, 0, slot_of(z)], h_send.at[r, 1], h_recv.at[r, 1], col_down)

    def send_own(r):
        send_up(r).start()
        send_down(r).start()

    def give(r, k, src, zs):
        return remote(src, xb.at[r, 1, slot_of(zs)], e_send.at[r, k], e_recv.at[r, k], across)

    def give_own(r):
        return give(r, 0, own_part(r), z)

    def give_down(r):
        return give(r, 1, xb.at[r, 0, slot_of(z_down)], z_down)

    def give_up(r):
        return give(r, 2, xb.at[r, 0, slot_of(z_up)], z_up)

    def give_far(r):
        return give(r, 3, xb.at[r, 0, slot_of(z_far)], z_far)

    def half_of(zs, i):
        return pl.ds(pl.multiple_of(zs * part + i * half, half), half)

    def pass_up(r):
        ref = xb.at[r, 0, half_of(z_down, 0)]
        return remote(ref, ref, z_send.at[r, 0], z_recv.at[r, 0], col_up)

    def pass_down(r):
        ref = xb.at[r, 0, half_of(z_up, 1)]
        return remote(ref, ref, z_send.at[r, 1], z_recv.at[r, 1], col_down)

    def up_near(r):
        ref = xb.at[r, 1, slot_of(z)]
        return remote(ref, ref, e_send.at[r, 1], e_recv.at[r, 1], col_up)

    def down_near(r):
        ref = xb.at[r, 1, slot_of(z)]
        return remote(ref, ref, e_send.at[r, 2], e_recv.at[r, 2], col_down)

    def up_far(r):
        ref = xb.at[r, 1, half_of(z_down, 0)]
        return remote(ref, ref, e_send.at[r, 3], e_recv.at[r, 3], col_up)

    def down_far(r):
        ref = xb.at[r, 1, half_of(z_up, 1)]
        return remote(ref, ref, e_send.at[r, 4], e_recv.at[r, 4], col_down)

    def near_blocks(r, across_too=True):
        arrived(xb.at[r, 0, slot_of(z_down)], h_recv.at[r, 0])
        pass_up(r).start()
        if across_too:
            give_down(r).start()
        arrived(xb.at[r, 0, slot_of(z_up)], h_recv.at[r, 1])
        pass_down(r).start()
        if across_too:
            give_up(r).start()

    def far_block(r, across_too=True):
        arrived(xb.at[r, 0, half_of(z_far, 0)], z_recv.at[r, 0])
        arrived(xb.at[r, 0, half_of(z_far, 1)], z_recv.at[r, 1])
        if across_too:
            give_far(r).start()

    def near_across(r):
        arrived(xb.at[r, 1, slot_of(z)], e_recv.at[r, 0])
        up_near(r).start()
        down_near(r).start()

    def far_across(r):
        arrived(xb.at[r, 1, slot_of(z_down)], e_recv.at[r, 1])
        up_far(r).start()
        arrived(xb.at[r, 1, slot_of(z_up)], e_recv.at[r, 2])
        down_far(r).start()

    def share(r):
        return remote(kv.at[r, 0], kv.at[r, 1], d_send.at[r], d_recv.at[r], sibling)

    def project(src, base, count):
        for j in range(0, 4 * width, 256):
            p = jnp.dot(src[...], w[:, j : j + 256], preferred_element_type=F32)
            pj[base : base + count, j : j + 256] = silu_of_double(0.5 * p).astype(BF16)

    def keys_values(r, across_too=True):
        if across_too:
            for k, zs in enumerate((z, z_down, z_up, z_far)):
                arrived(xb.at[r, 1, slot_of(zs)], e_recv.at[r, k])
        else:
            for k in range(2):
                arrived(xb.at[r, 1, half_of(z_far, k)], e_recv.at[r, 3 + k])
        block_rows = xb[r].reshape(mine, width)
        for j in range(0, 2 * width, 256):
            start = width + j if j < width else 2 * width + j
            p = jnp.dot(block_rows, w[:, start : start + 256], preferred_element_type=F32)
            kv[r, 0, :, j : j + 256] = silu_of_double(0.5 * p).astype(BF16)
        share(r).start()

    def attend(r, base, count, mask_row):
        for h in range(HEADS):
            cols = slice(h * head, (h + 1) * head)
            key_cols = slice(width + h * head, width + (h + 1) * head)
            keys = kv[r, :, :, key_cols].reshape(2 * mine, head)
            values = kv[r, :, :, cols].reshape(2 * mine, head)
            q = pj[base : base + count, 2 * width + h * head : 2 * width + (h + 1) * head]
            s = lax.dot_general(q, keys, (((1,), (1,)), ((), ())), preferred_element_type=F32)
            if mask_row is None:
                t = jnp.concatenate(
                    [s[:rows] * mb[r, 0:1, :], s[rows:] * mb[r, 1:2, :]], axis=0
                )
            else:
                t = s * mb[r, mask_row : mask_row + 1, :]
            weights = silu_of_double(t).astype(BF16)
            acc[base : base + count, cols] += jnp.dot(weights, values, preferred_element_type=F32)

    last = ROUNDS - 1
    for r in range(ROUNDS):
        arrived(own_part(r), hb_recv.at[r])
        if r < AHEAD:
            send_own(r)
        give_own(r).start()
        xb[r, 0, slot_of(z), :] = hb[r * part : (r + 1) * part, :]

    @pl.when(swapped == 1)
    def _():
        cb_remote.start()
        mb_remote.start()

    w_copy.wait()
    project(hb, 0, rows)
    near_blocks(0)
    send_own(AHEAD)

    tri = lax.broadcasted_iota(jnp.int32, (rows, rows), 1) <= lax.broadcasted_iota(
        jnp.int32, (rows, rows), 0
    )
    for h in range(HEADS):
        cols = slice(h * head, (h + 1) * head)
        q = pj[0:rows, 2 * width + h * head : 2 * width + (h + 1) * head]
        k = pj[0:rows, 3 * width + h * head : 3 * width + (h + 1) * head]
        v = pj[0:rows, width + h * head : width + (h + 1) * head]
        s = lax.dot_general(q, k, (((1,), (1,)), ((), ())), preferred_element_type=F32)
        t = jnp.where(tri, s * half_scale, 0.0)
        acc[0:rows, cols] = jnp.dot(
            silu_of_double(t).astype(BF16), v, preferred_element_type=F32
        )

    near_blocks(1)
    send_own(AHEAD + 1)
    far_block(0)
    arrived(cb, cb_recv)
    project(cb, rows, cands)
    near_blocks(2)
    send_own(AHEAD + 2)
    far_block(1)
    for h in range(HEADS):
        cols = slice(h * head, (h + 1) * head)
        q = pj[rows:, 2 * width + h * head : 2 * width + (h + 1) * head].astype(F32)
        k = pj[rows:, 3 * width + h * head : 3 * width + (h + 1) * head].astype(F32)
        v = pj[rows:, width + h * head : width + (h + 1) * head].astype(F32)
        t = jnp.sum(q * k, axis=1, keepdims=True) * half_scale
        acc[rows:, cols] = silu_of_double(t).astype(BF16).astype(F32) * v
    arrived(mb, mb_recv)
    keys_values(0)
    arrived(ow_other, ow_recv.at[0])
    for copy in ow_second:
        copy.start()

    @pl.loop(1, last)
    def _(r):
        @pl.when(r + 2 < last)
        def _():
            near_blocks(r + 2)

        @pl.when(r + 2 + AHEAD < ROUNDS)
        def _():
            send_own(r + 2 + AHEAD)

        @pl.when(r + 2 == last)
        def _():
            near_blocks(last, False)
            near_across(last)

        @pl.when(r + 1 < last)
        def _():
            far_block(r + 1)

        @pl.when(r + 1 == last)
        def _():
            far_block(last, False)
            far_across(last)

        keys_values(r)
        arrived(kv.at[r - 1, 1], d_recv.at[r - 1])
        attend(r - 1, 0, rows + cands, None)

    keys_values(last, False)
    arrived(kv.at[last - 1, 1], d_recv.at[last - 1])
    attend(last - 1, 0, rows + cands, None)
    for i in range(3):
        yy = lax.rem(y + 3 - i, 4)
        arrived(ow_from(zlo, yy), ow_recv.at[1 + i])
        arrived(ow_from(1 - zlo, yy), ow_recv.at[4 + i])
    ow_own.wait()
    ow_third.start()

    def finish(base, count):
        for j in range(base, base + count, 64):
            rows_of = slice(j, j + 64)
            gate = pj[rows_of, 0:width].astype(F32)
            gated[rows_of, :] = (layer_norm(acc[rows_of, :]) * gate).astype(BF16)

    arrived(kv.at[last, 1], d_recv.at[last])
    attend(last, 0, rows, 0)
    finish(0, rows)
    arrived(ow.at[:, 1 - core], ow_recv.at[7])

    def branch(base, count, j):
        weight = ow[:, :, :, j : j + 256].reshape(width, 256)
        return jnp.dot(gated[base : base + count, :], weight, preferred_element_type=F32)

    row_live = lax.broadcasted_iota(jnp.int32, (rows, 256), 0).astype(F32) < mb[0, 2:3, 0:256]
    for j in range(0, width, 256):
        mixed = hb[:, j : j + 256].astype(F32) + branch(0, rows, j)
        stage[:, j : j + 256] = jnp.where(row_live, mixed, 0.0).astype(BF16)

    hist_back = remote(stage, hist_out.at[0], ret_send.at[0], ret_recv.at[0], swap)

    @pl.when(swapped == 1)
    def _():
        hist_back.start()

    @pl.when(swapped == 0)
    def _():
        pltpu.make_async_copy(stage, hist_out.at[0], ret_recv.at[0]).start()

    attend(last, rows, cands, 1)
    finish(rows, cands)
    for j in range(0, width, 256):
        mixed = cb[:, j : j + 256].astype(F32) + branch(rows, cands, j)
        cb[:, j : j + 256] = mixed.astype(BF16)
    lbuf[...] = lax.dot_general(
        task_t[...], cb[...], (((1,), (1,)), ((), ())), preferred_element_type=F32
    )
    logits_back = remote(lbuf, lback, ret_send.at[1], ret_recv.at[1], swap)

    @pl.when(swapped == 1)
    def _():
        logits_back.start()

    @pl.when(swapped == 0)
    def _():
        pltpu.make_async_copy(lbuf, lback, ret_recv.at[1]).start()

    @pl.loop(0, ROUNDS)
    def _(r):
        send_up(r).wait_send()
        send_down(r).wait_send()
        pass_up(r).wait_send()
        pass_down(r).wait_send()
        give_own(r).wait_send()
        share(r).wait_send()

        @pl.when(r < last)
        def _():
            give_down(r).wait_send()
            give_up(r).wait_send()
            give_far(r).wait_send()

    up_near(last).wait_send()
    down_near(last).wait_send()
    up_far(last).wait_send()
    down_far(last).wait_send()

    for copy in (*ow_first, *ow_second, ow_third):
        copy.wait_send()

    @pl.when(swapped == 1)
    def _():
        for r in range(ROUNDS):
            fetch_remote(r).wait_send()
        cb_remote.wait_send()
        mb_remote.wait_send()
        hist_back.wait_send()
        logits_back.wait_send()

    arrived(lback, ret_recv.at[1])
    task_id = lax.broadcasted_iota(jnp.int32, lback.shape, 0)
    picked = jnp.sum(jnp.where(task_id == targets[...], lback[...], 0.0), axis=0, keepdims=True)
    logprob[...] = jnp.minimum(picked, 0.0) - jnp.log1p(jnp.exp(-jnp.abs(picked)))
    arrived(hist_out.at[0], ret_recv.at[0])


def local(
    history, candidates, lengths, block_order, targets, projection, output_weight, task_weight
):
    rows, width = history.shape[1], history.shape[2]
    cands = candidates.shape[1]
    tasks = task_weight.shape[1]
    part = rows // ROUNDS
    mine = 8 * part
    any_space = pl.BlockSpec(memory_space=pl.ANY)
    smem = pl.BlockSpec(memory_space=pltpu.SMEM)
    vmem = pl.BlockSpec(memory_space=pltpu.VMEM)
    dma = pltpu.SemaphoreType.DMA
    return pl.pallas_call(
        kernel,
        out_shape=(
            jax.ShapeDtypeStruct((1, rows, width), BF16),
            jax.ShapeDtypeStruct((1, cands), F32),
        ),
        in_specs=[any_space, any_space, smem, smem, vmem, any_space, any_space, vmem],
        out_specs=(any_space, vmem),
        scratch_shapes=[
            pltpu.VMEM((width, 4 * width), BF16),
            pltpu.VMEM((8, 2, width // 16, width), BF16),
            pltpu.VMEM((rows, width), BF16),
            pltpu.VMEM((cands, width), BF16),
            pltpu.VMEM((ROUNDS, 2, 4 * part, width), BF16),
            pltpu.VMEM((ROUNDS, 2, mine, 2 * width), BF16),
            pltpu.VMEM((rows + cands, 4 * width), BF16),
            pltpu.VMEM((rows + cands, width), F32),
            pltpu.VMEM((rows + cands, width), BF16),
            pltpu.VMEM((rows, width), BF16),
            pltpu.VMEM((ROUNDS, 8, 2 * mine), F32),
            pltpu.VMEM((ROUNDS, 8, 2 * mine), F32),
            pltpu.VMEM((tasks, cands), F32),
            pltpu.VMEM((tasks, cands), F32),
            dma, dma((ROUNDS,)), dma((ROUNDS,)), dma, dma, dma, dma,
            dma((ROUNDS, 2)), dma((ROUNDS, 2)),
            dma((ROUNDS, 2)), dma((ROUNDS, 2)),
            dma((ROUNDS, 5)), dma((ROUNDS, 5)),
            dma((ROUNDS,)), dma((ROUNDS,)),
            dma((8,)), dma((8,)), dma,
            dma((2,)), dma((2,)),
        ],
        compiler_params=pltpu.CompilerParams(
            collective_id=0, has_side_effects=True, vmem_limit_bytes=56 * 2**20
        ),
    )(
        history, candidates, lengths[None, :], block_order, targets, projection, output_weight,
        task_weight.T,
    )


def solution(mesh):
    in_specs = (
        P("grp", "ctx", None),
        P("grp", "ctx", None),
        P("grp"),
        P("grp", None),
        P("grp", "ctx"),
        P(),
        P("grp", None),
        P(),
    )
    out_specs = (P("grp", "ctx", None), P("grp", "ctx"))
    return jax.shard_map(local, mesh=mesh, in_specs=in_specs, out_specs=out_specs, check_vma=False)
```

```python
import functools

import jax
import jax.numpy as jnp
from jax import lax
from jax.experimental import pallas as pl
from jax.experimental.pallas import tpu as pltpu
from jax.sharding import PartitionSpec as P

HEADS = 8
NORM_EPS = 1e-05
ROUNDS = 6
AHEAD = 2
F32, BF16 = jnp.float32, jnp.bfloat16
MESH = pl.DeviceIdType.MESH


def silu_of_double(half):
    return half + half * jnp.tanh(half)


def layer_norm(mixed):
    centre = mixed - jnp.mean(mixed, axis=-1, keepdims=True)
    spread = jnp.mean(centre * centre, axis=-1, keepdims=True)
    return centre * lax.rsqrt(spread + NORM_EPS)


def kernel(
    hist, cand, lengths, order, targets, proj, out_weight, task_t,
    hist_out, logprob,
    w, ow, hb, cb, xb, kv, pj, acc, gated, stage, mloc, mb, lbuf, lback,
    w_sem, hb_send, hb_recv, cb_send, cb_recv, mb_send, mb_recv,
    h_send, h_recv, z_send, z_recv, e_send, e_recv, d_send, d_recv,
    ow_send, ow_recv, ow_local, ret_send, ret_recv,
):
    rows = hb.shape[0]
    cands = cb.shape[0]
    width = hb.shape[1]
    part = rows // ROUNDS
    half = part // 2
    column = 4 * part
    mine = 2 * column
    head = width // HEADS
    half_scale = 0.5 * head ** (-0.5)

    g = lax.axis_index("grp")
    c = lax.axis_index("ctx")
    core = lax.rem(g, 2)
    pair = g - core
    zlo = g // 8
    y = lax.rem(g // 2, 4)
    x = c // 4
    z = lax.rem(c, 4)
    swapped = lax.rem(x // 2 + core, 2)
    home_core = lax.rem(core + swapped, 2)
    home_x = x + swapped * (3 - 2 * x)
    z_up = lax.rem(z + 1, 4)
    z_down = lax.rem(z + 3, 4)
    z_far = lax.rem(z + 2, 4)

    swap = (pair + home_core, home_x * 4 + z)
    col_up = (g, x * 4 + z_up)
    col_down = (g, x * 4 + z_down)
    across = (g, (x + 1 - 2 * lax.rem(x, 2)) * 4 + z)
    sibling = (pair + 1 - core, c)
    z_pair = ((1 - zlo) * 8 + y * 2 + core, c)
    y_others = [(zlo * 8 + lax.rem(y + i, 4) * 2 + core, c) for i in (1, 2, 3)]

    def remote(src, dst, send, recv, to):
        return pltpu.make_async_remote_copy(
            src_ref=src, dst_ref=dst, send_sem=send, recv_sem=recv, device_id=to, device_id_type=MESH
        )

    def arrived(ref, sem):
        pltpu.make_async_copy(ref, ref, sem).wait()

    barrier = pltpu.get_barrier_semaphore()
    greeted = [col_up, col_down, across, sibling, z_pair, *y_others]
    for other in greeted:
        pl.semaphore_signal(barrier, inc=1, device_id=other, device_id_type=MESH)

    @pl.when(swapped == 1)
    def _():
        pl.semaphore_signal(barrier, inc=1, device_id=swap, device_id_type=MESH)

    w_copy = pltpu.make_async_copy(proj, w, w_sem)
    w_copy.start()
    ow_own = pltpu.make_async_copy(out_weight, ow.at[zlo * 4 + y, core], ow_local)
    ow_own.start()

    lane = lax.broadcasted_iota(jnp.int32, (8, 2 * mine), 1)
    slot = lane // part
    own_block = order[0, c]
    limit = lengths[0, 0]
    block = jnp.zeros_like(lane)
    x_pair = x + 1 - 2 * lax.rem(x, 2)
    columns = (x, x_pair, 3 - x, 3 - x_pair)
    for i, source in enumerate(columns):
        for zs in range(4):
            block = jnp.where(slot == 4 * i + zs, order[0, source * 4 + zs], block)
    row_id = lax.broadcasted_iota(jnp.int32, (8, 2 * mine), 0)
    first = block * rows + lax.rem(lane, part)
    causal = jnp.where(row_id == 0, block, -1) < own_block
    own_live = (limit - own_block * rows).astype(F32)
    for r in range(ROUNDS):
        live = first + r * part < limit
        mloc[r] = jnp.where(row_id == 2, own_live, jnp.where(live & causal, half_scale, 0.0))

    pl.semaphore_wait(barrier, len(greeted) + swapped)

    def slot_of(zs):
        return pl.ds(pl.multiple_of(zs * part, part), part)

    def part_of(r):
        return pl.ds(pl.multiple_of(r * part, part), part)

    def fetch_remote(r):
        return remote(hist.at[0, part_of(r)], hb.at[part_of(r)], hb_send.at[r], hb_recv.at[r], swap)

    cb_remote = remote(cand.at[0], cb, cb_send, cb_recv, swap)
    mb_remote = remote(mloc, mb, mb_send, mb_recv, swap)

    @pl.when(swapped == 1)
    def _():
        for r in range(ROUNDS):
            fetch_remote(r).start()

    @pl.when(swapped == 0)
    def _():
        for r in range(ROUNDS):
            pltpu.make_async_copy(hist.at[0, part_of(r)], hb.at[part_of(r)], hb_recv.at[r]).start()
        pltpu.make_async_copy(cand.at[0], cb, cb_recv).start()
        pltpu.make_async_copy(mloc, mb, mb_recv).start()

    ow_mine = out_weight
    ow_slot = ow.at[zlo * 4 + y, core]
    ow_first = [remote(ow_mine, ow_slot, ow_send.at[0], ow_recv.at[0], z_pair)]
    for i in range(3):
        ow_first.append(remote(ow_mine, ow_slot, ow_send.at[1 + i], ow_recv.at[1 + i], y_others[i]))
    for copy in ow_first:
        copy.start()

    def ow_from(zl, yy):
        return ow.at[zl * 4 + yy, core]

    ow_other = ow_from(1 - zlo, y)
    ow_second = [
        remote(ow_other, ow_other, ow_send.at[4 + i], ow_recv.at[4 + i], y_others[i]) for i in range(3)
    ]
    ow_third = remote(ow.at[:, core], ow.at[:, core], ow_send.at[7], ow_recv.at[7], sibling)

    def own_part(r):
        return hb.at[part_of(r)]

    def send_up(r):
        return remote(own_part(r), xb.at[r, 0, slot_of(z)], h_send.at[r, 0], h_recv.at[r, 0], col_up)

    def send_down(r):
        return remote(own_part(r), xb.at[r, 0, slot_of(z)], h_send.at[r, 1], h_recv.at[r, 1], col_down)

    def send_own(r):
        send_up(r).start()
        send_down(r).start()

    def give(r, k, src, zs):
        return remote(src, xb.at[r, 1, slot_of(zs)], e_send.at[r, k], e_recv.at[r, k], across)

    def give_own(r):
        return give(r, 0, own_part(r), z)

    def give_down(r):
        return give(r, 1, xb.at[r, 0, slot_of(z_down)], z_down)

    def give_up(r):
        return give(r, 2, xb.at[r, 0, slot_of(z_up)], z_up)

    def give_far(r):
        return give(r, 3, xb.at[r, 0, slot_of(z_far)], z_far)

    def half_of(zs, i):
        return pl.ds(pl.multiple_of(zs * part + i * half, half), half)

    def pass_up(r):
        ref = xb.at[r, 0, half_of(z_down, 0)]
        return remote(ref, ref, z_send.at[r, 0], z_recv.at[r, 0], col_up)

    def pass_down(r):
        ref = xb.at[r, 0, half_of(z_up, 1)]
        return remote(ref, ref, z_send.at[r, 1], z_recv.at[r, 1], col_down)

    def up_near(r):
        ref = xb.at[r, 1, slot_of(z)]
        return remote(ref, ref, e_send.at[r, 1], e_recv.at[r, 1], col_up)

    def down_near(r):
        ref = xb.at[r, 1, slot_of(z)]
        return remote(ref, ref, e_send.at[r, 2], e_recv.at[r, 2], col_down)

    def up_far(r):
        ref = xb.at[r, 1, half_of(z_down, 0)]
        return remote(ref, ref, e_send.at[r, 3], e_recv.at[r, 3], col_up)

    def down_far(r):
        ref = xb.at[r, 1, half_of(z_up, 1)]
        return remote(ref, ref, e_send.at[r, 4], e_recv.at[r, 4], col_down)

    def near_blocks(r, across_too=True):
        arrived(xb.at[r, 0, slot_of(z_down)], h_recv.at[r, 0])
        pass_up(r).start()
        if across_too:
            give_down(r).start()
        arrived(xb.at[r, 0, slot_of(z_up)], h_recv.at[r, 1])
        pass_down(r).start()
        if across_too:
            give_up(r).start()

    def far_block(r, across_too=True):
        arrived(xb.at[r, 0, half_of(z_far, 0)], z_recv.at[r, 0])
        arrived(xb.at[r, 0, half_of(z_far, 1)], z_recv.at[r, 1])
        if across_too:
            give_far(r).start()

    def near_across(r):
        arrived(xb.at[r, 1, slot_of(z)], e_recv.at[r, 0])
        up_near(r).start()
        down_near(r).start()

    def far_across(r):
        arrived(xb.at[r, 1, slot_of(z_down)], e_recv.at[r, 1])
        up_far(r).start()
        arrived(xb.at[r, 1, slot_of(z_up)], e_recv.at[r, 2])
        down_far(r).start()

    def share(r):
        return remote(kv.at[r, 0], kv.at[r, 1], d_send.at[r], d_recv.at[r], sibling)

    def project(src, base, count):
        for j in range(0, 4 * width, 256):
            p = jnp.dot(src[...], w[:, j : j + 256], preferred_element_type=F32)
            pj[base : base + count, j : j + 256] = silu_of_double(0.5 * p).astype(BF16)

    def keys_values(r, across_too=True):
        if across_too:
            for k, zs in enumerate((z, z_down, z_up, z_far)):
                arrived(xb.at[r, 1, slot_of(zs)], e_recv.at[r, k])
        else:
            for k in range(2):
                arrived(xb.at[r, 1, half_of(z_far, k)], e_recv.at[r, 3 + k])
        block_rows = xb[r].reshape(mine, width)
        for j in range(0, 2 * width, 256):
            start = width + j if j < width else 2 * width + j
            p = jnp.dot(block_rows, w[:, start : start + 256], preferred_element_type=F32)
            kv[r, 0, :, j : j + 256] = silu_of_double(0.5 * p).astype(BF16)
        share(r).start()

    def attend(r, base, count, mask_row):
        for h in range(HEADS):
            cols = slice(h * head, (h + 1) * head)
            key_cols = slice(width + h * head, width + (h + 1) * head)
            keys = kv[r, :, :, key_cols].reshape(2 * mine, head)
            values = kv[r, :, :, cols].reshape(2 * mine, head)
            q = pj[base : base + count, 2 * width + h * head : 2 * width + (h + 1) * head]
            s = lax.dot_general(q, keys, (((1,), (1,)), ((), ())), preferred_element_type=F32)
            if mask_row is None:
                t = jnp.concatenate(
                    [s[:rows] * mb[r, 0:1, :], s[rows:] * mb[r, 1:2, :]], axis=0
                )
            else:
                t = s * mb[r, mask_row : mask_row + 1, :]
            weights = silu_of_double(t).astype(BF16)
            acc[base : base + count, cols] += jnp.dot(weights, values, preferred_element_type=F32)

    last = ROUNDS - 1
    for r in range(ROUNDS):
        arrived(own_part(r), hb_recv.at[r])
        if r < AHEAD:
            send_own(r)
        give_own(r).start()
        xb[r, 0, slot_of(z), :] = hb[r * part : (r + 1) * part, :]

    @pl.when(swapped == 1)
    def _():
        cb_remote.start()
        mb_remote.start()

    w_copy.wait()
    project(hb, 0, rows)
    near_blocks(0)
    send_own(AHEAD)

    tri = lax.broadcasted_iota(jnp.int32, (rows, rows), 1) <= lax.broadcasted_iota(
        jnp.int32, (rows, rows), 0
    )
    for h in range(HEADS):
        cols = slice(h * head, (h + 1) * head)
        q = pj[0:rows, 2 * width + h * head : 2 * width + (h + 1) * head]
        k = pj[0:rows, 3 * width + h * head : 3 * width + (h + 1) * head]
        v = pj[0:rows, width + h * head : width + (h + 1) * head]
        s = lax.dot_general(q, k, (((1,), (1,)), ((), ())), preferred_element_type=F32)
        t = jnp.where(tri, s * half_scale, 0.0)
        acc[0:rows, cols] = jnp.dot(
            silu_of_double(t).astype(BF16), v, preferred_element_type=F32
        )

    near_blocks(1)
    send_own(AHEAD + 1)
    far_block(0)
    near_blocks(2)
    send_own(AHEAD + 2)
    far_block(1)
    keys_values(0)
    arrived(cb, cb_recv)
    project(cb, rows, cands)
    for h in range(HEADS):
        cols = slice(h * head, (h + 1) * head)
        q = pj[rows:, 2 * width + h * head : 2 * width + (h + 1) * head].astype(F32)
        k = pj[rows:, 3 * width + h * head : 3 * width + (h + 1) * head].astype(F32)
        v = pj[rows:, width + h * head : width + (h + 1) * head].astype(F32)
        t = jnp.sum(q * k, axis=1, keepdims=True) * half_scale
        acc[rows:, cols] = silu_of_double(t).astype(BF16).astype(F32) * v
    arrived(mb, mb_recv)
    arrived(ow_other, ow_recv.at[0])
    for copy in ow_second:
        copy.start()

    @pl.loop(1, last)
    def _(r):
        @pl.when(r + 2 < last)
        def _():
            near_blocks(r + 2)

        @pl.when(r + 2 + AHEAD < ROUNDS)
        def _():
            send_own(r + 2 + AHEAD)

        @pl.when(r + 2 == last)
        def _():
            near_blocks(last, False)
            near_across(last)

        @pl.when(r + 1 < last)
        def _():
            far_block(r + 1)

        @pl.when(r + 1 == last)
        def _():
            far_block(last, False)
            far_across(last)

        keys_values(r)
        arrived(kv.at[r - 1, 1], d_recv.at[r - 1])
        attend(r - 1, 0, rows + cands, None)

    keys_values(last, False)
    arrived(kv.at[last - 1, 1], d_recv.at[last - 1])
    attend(last - 1, 0, rows + cands, None)
    for i in range(3):
        yy = lax.rem(y + 3 - i, 4)
        arrived(ow_from(zlo, yy), ow_recv.at[1 + i])
        arrived(ow_from(1 - zlo, yy), ow_recv.at[4 + i])
    ow_own.wait()
    ow_third.start()

    def finish(base, count):
        for j in range(base, base + count, 64):
            rows_of = slice(j, j + 64)
            gate = pj[rows_of, 0:width].astype(F32)
            gated[rows_of, :] = (layer_norm(acc[rows_of, :]) * gate).astype(BF16)

    arrived(kv.at[last, 1], d_recv.at[last])
    attend(last, 0, rows, 0)
    finish(0, rows)
    arrived(ow.at[:, 1 - core], ow_recv.at[7])

    def branch(base, count, j):
        weight = ow[:, :, :, j : j + 256].reshape(width, 256)
        return jnp.dot(gated[base : base + count, :], weight, preferred_element_type=F32)

    row_live = lax.broadcasted_iota(jnp.int32, (rows, 256), 0).astype(F32) < mb[0, 2:3, 0:256]
    for j in range(0, width, 256):
        mixed = hb[:, j : j + 256].astype(F32) + branch(0, rows, j)
        stage[:, j : j + 256] = jnp.where(row_live, mixed, 0.0).astype(BF16)

    hist_back = remote(stage, hist_out.at[0], ret_send.at[0], ret_recv.at[0], swap)

    @pl.when(swapped == 1)
    def _():
        hist_back.start()

    @pl.when(swapped == 0)
    def _():
        pltpu.make_async_copy(stage, hist_out.at[0], ret_recv.at[0]).start()

    attend(last, rows, cands, 1)
    finish(rows, cands)
    for j in range(0, width, 256):
        mixed = cb[:, j : j + 256].astype(F32) + branch(rows, cands, j)
        cb[:, j : j + 256] = mixed.astype(BF16)
    lbuf[...] = lax.dot_general(
        task_t[...], cb[...], (((1,), (1,)), ((), ())), preferred_element_type=F32
    )
    logits_back = remote(lbuf, lback, ret_send.at[1], ret_recv.at[1], swap)

    @pl.when(swapped == 1)
    def _():
        logits_back.start()

    @pl.when(swapped == 0)
    def _():
        pltpu.make_async_copy(lbuf, lback, ret_recv.at[1]).start()

    @pl.loop(0, ROUNDS)
    def _(r):
        send_up(r).wait_send()
        send_down(r).wait_send()
        pass_up(r).wait_send()
        pass_down(r).wait_send()
        give_own(r).wait_send()
        share(r).wait_send()

        @pl.when(r < last)
        def _():
            give_down(r).wait_send()
            give_up(r).wait_send()
            give_far(r).wait_send()

    up_near(last).wait_send()
    down_near(last).wait_send()
    up_far(last).wait_send()
    down_far(last).wait_send()

    for copy in (*ow_first, *ow_second, ow_third):
        copy.wait_send()

    @pl.when(swapped == 1)
    def _():
        for r in range(ROUNDS):
            fetch_remote(r).wait_send()
        cb_remote.wait_send()
        mb_remote.wait_send()
        hist_back.wait_send()
        logits_back.wait_send()

    arrived(lback, ret_recv.at[1])
    task_id = lax.broadcasted_iota(jnp.int32, lback.shape, 0)
    picked = jnp.sum(jnp.where(task_id == targets[...], lback[...], 0.0), axis=0, keepdims=True)
    logprob[...] = jnp.minimum(picked, 0.0) - jnp.log1p(jnp.exp(-jnp.abs(picked)))
    arrived(hist_out.at[0], ret_recv.at[0])


def local(
    history, candidates, lengths, block_order, targets, projection, output_weight, task_weight
):
    rows, width = history.shape[1], history.shape[2]
    cands = candidates.shape[1]
    tasks = task_weight.shape[1]
    part = rows // ROUNDS
    mine = 8 * part
    any_space = pl.BlockSpec(memory_space=pl.ANY)
    smem = pl.BlockSpec(memory_space=pltpu.SMEM)
    vmem = pl.BlockSpec(memory_space=pltpu.VMEM)
    dma = pltpu.SemaphoreType.DMA
    return pl.pallas_call(
        kernel,
        out_shape=(
            jax.ShapeDtypeStruct((1, rows, width), BF16),
            jax.ShapeDtypeStruct((1, cands), F32),
        ),
        in_specs=[any_space, any_space, smem, smem, vmem, any_space, any_space, vmem],
        out_specs=(any_space, vmem),
        scratch_shapes=[
            pltpu.VMEM((width, 4 * width), BF16),
            pltpu.VMEM((8, 2, width // 16, width), BF16),
            pltpu.VMEM((rows, width), BF16),
            pltpu.VMEM((cands, width), BF16),
            pltpu.VMEM((ROUNDS, 2, 4 * part, width), BF16),
            pltpu.VMEM((ROUNDS, 2, mine, 2 * width), BF16),
            pltpu.VMEM((rows + cands, 4 * width), BF16),
            pltpu.VMEM((rows + cands, width), F32),
            pltpu.VMEM((rows + cands, width), BF16),
            pltpu.VMEM((rows, width), BF16),
            pltpu.VMEM((ROUNDS, 8, 2 * mine), F32),
            pltpu.VMEM((ROUNDS, 8, 2 * mine), F32),
            pltpu.VMEM((tasks, cands), F32),
            pltpu.VMEM((tasks, cands), F32),
            dma, dma((ROUNDS,)), dma((ROUNDS,)), dma, dma, dma, dma,
            dma((ROUNDS, 2)), dma((ROUNDS, 2)),
            dma((ROUNDS, 2)), dma((ROUNDS, 2)),
            dma((ROUNDS, 5)), dma((ROUNDS, 5)),
            dma((ROUNDS,)), dma((ROUNDS,)),
            dma((8,)), dma((8,)), dma,
            dma((2,)), dma((2,)),
        ],
        compiler_params=pltpu.CompilerParams(
            collective_id=0, has_side_effects=True, vmem_limit_bytes=56 * 2**20
        ),
    )(
        history, candidates, lengths[None, :], block_order, targets, projection, output_weight,
        task_weight.T,
    )


def solution(mesh):
    in_specs = (
        P("grp", "ctx", None),
        P("grp", "ctx", None),
        P("grp"),
        P("grp", None),
        P("grp", "ctx"),
        P(),
        P("grp", None),
        P(),
    )
    out_specs = (P("grp", "ctx", None), P("grp", "ctx"))
    return jax.shard_map(local, mesh=mesh, in_specs=in_specs, out_specs=out_specs, check_vma=False)
```
